512 devices in a mesh: lon: 8 (over y, z_hi), mem: 64 (over x, z_lo, core).
Axes of the slice: x: 4, y: 4, z: 16 (z_hi: 2, z_lo: 8; z = z_hi * 8 + z_lo), core: 2. Of those that a mesh axis runs over, the one named last changes fastest.
Arguments:
- ensemble: float32 [64, 98304], P('mem', 'lon')
- increments: bfloat16 [64, 98304], P('mem', 'lon'), may hold values from -6 to 6
- offsets: int32 [192, 7], P('lon'), may hold values from -12 to 12, as said below
- taper: bfloat16 [8, 512, 512], replicated
Outputs:
- covariance_product: float32 [64, 98304], P('mem', 'lon')
The draws below stay inside these ranges and needn't reach their ends.
Inputs may be any that keep to these rules, and one draw needn't show every extreme that they name: Each row lists 7 different nonzero offsets in ascending order.
All inputs are finite; a program needn't handle non-finite values.
Results may differ from the reference program's by a relative error of at most 0.008.
Values may be sent and summed in bfloat16 or wider, within the bound.
A program may use at most 64 MiB of HBM per device.

```python
import math
import jax
import jax.numpy as jnp
from jax import lax

BLOCK = 512
BLOCKS_DEV = 24
NEIGHBORS = 7
MEMBERS = 64
INCREMENTS = 64
NBLOCKS = 192
COLUMNS = 98304


def draw_ensemble(key, part):
    key_noise, key_column, key_background = jax.random.split(key, 3)
    member_index = jnp.arange(MEMBERS, dtype=jnp.float32)[:, None]
    member_scale = 0.5 * 3.2 ** (member_index / max(MEMBERS - 1, 1))
    column_scale = jnp.exp(jax.random.uniform(key_column, (1, COLUMNS), jnp.float32, math.log(0.5), math.log(1.5)))
    background = 24.0 * jax.random.normal(key_background, (1, COLUMNS), jnp.float32)
    spread = jnp.clip(jax.random.normal(key_noise, (MEMBERS, COLUMNS), jnp.float32), -5.0, 5.0)
    return (background + member_scale * column_scale * spread).astype(jnp.float32)


def draw_taper(key, part):
    fresh = jnp.clip(jax.random.normal(key, (NEIGHBORS + 1, BLOCK, BLOCK), jnp.float32), -5.0, 5.0)
    slot_index = jnp.arange(NEIGHBORS + 1)[:, None, None]
    identity = jnp.eye(BLOCK, dtype=jnp.float32)[None, :, :]
    tiles = jnp.where(slot_index == 0, identity + 0.4 / math.sqrt(BLOCK) * fresh, 0.5 / math.sqrt(BLOCK) * fresh)
    return tiles.astype(jnp.bfloat16)


def draw_offsets(key, part):
    reach_blocks = BLOCKS_DEV // 2
    choices_all = jnp.concatenate([jnp.arange(-reach_blocks, 0, dtype=jnp.int32), jnp.arange(1, reach_blocks + 1, dtype=jnp.int32)])
    width_all = 2 * reach_blocks
    row_keys = jax.random.split(key, NBLOCKS)
    position = jnp.arange(width_all, dtype=jnp.int32)
    extremes = (position == 0) | (position == width_all - 1)

    def single_row(row_key, row_number):
        shuffled = jax.random.permutation(row_key, width_all).astype(jnp.int32)
        ranking = jnp.argsort(shuffled).astype(jnp.int32)
        ranking = jnp.where((row_number == 0) & extremes, ranking - width_all, ranking)
        ordering = jnp.argsort(ranking)
        return jnp.sort(choices_all[ordering[:NEIGHBORS]])
    return jax.vmap(single_row)(row_keys, jnp.arange(NBLOCKS, dtype=jnp.int32)).astype(jnp.int32)


def shard_levels(stream_key, extent, pieces, least, top_value):
    loudness = 1.0
    for dim, parts in pieces:
        steps = jax.random.uniform(jax.random.fold_in(jax.random.fold_in(stream_key, 6), dim), (parts,), jnp.float32, least / len(pieces), top_value / len(pieces))
        loudness = loudness * jnp.repeat(jnp.exp(steps), extent[dim] // parts).reshape((-1,) + (1,) * (len(extent) - 1 - dim))
    return loudness


def normal_values(key, dims, scale, most, cuts=(), kind=jnp.bfloat16):
    result = jax.random.normal(key, dims, jnp.float32) * scale
    if len(cuts) > 0:
        result = shard_levels(key, dims, cuts, -0.22, 0.18) * result
    return jnp.clip(result, min=-most, max=most).astype(kind)


def setup_inputs(seed: int = 0) -> dict:
    key_of = jax.random.split(jax.random.key(seed), 5)
    ensemble = draw_ensemble(jax.random.fold_in(key_of[4], 71), 0)
    increments = normal_values(key_of[1], (INCREMENTS, COLUMNS), 1.0, 6.0, ((0, 64), (1, 8)))
    offsets = draw_offsets(jax.random.fold_in(key_of[4], 71), 0)
    taper = draw_taper(jax.random.fold_in(key_of[4], 71), 0)
    return {"ensemble": ensemble, "increments": increments, "offsets": offsets, "taper": taper}


def taper_apply(weighted, offsets, taper):
    vectors = weighted.shape[0]
    block_count = offsets.shape[0]
    blocks = weighted.reshape(vectors, block_count, BLOCK)
    block_rows = jnp.arange(block_count, dtype=jnp.int32)
    indices = jnp.concatenate([block_rows[:, None], (block_rows[:, None] + offsets) % block_count], axis=1).astype(jnp.int32)
    picked = jnp.take(blocks, indices, axis=1)
    tapered = jnp.einsum("qrsb,sab->qra", picked.astype(jnp.float32), taper.astype(jnp.float32))
    return tapered.reshape(vectors, block_count * BLOCK)


def reference(ensemble, increments, offsets, taper):
    ens_mean = jnp.sum(ensemble, axis=0) / MEMBERS
    perturb = (ensemble - ens_mean[None, :]).astype(jnp.bfloat16)

    def accumulate(member, summed):
        member_row = lax.dynamic_index_in_dim(perturb, member, 0, keepdims=False).astype(jnp.float32)
        weighted = (member_row[None, :] * increments.astype(jnp.float32)).astype(jnp.bfloat16)
        tapered = taper_apply(weighted, offsets, taper)
        return summed + member_row[None, :] * tapered

    summed = lax.fori_loop(0, MEMBERS, accumulate, jnp.zeros((INCREMENTS, COLUMNS), jnp.float32))
    return summed / (MEMBERS - 1)
```

```python
import functools

import jax
import jax.numpy as jnp
from jax import lax
from jax.experimental import pallas as pl
from jax.experimental.pallas import tpu as pltpu
from jax.sharding import PartitionSpec as P

MESH = pl.DeviceIdType.MESH
F32, BF16 = jnp.float32, jnp.bfloat16
NT = (((1,), (1,)), ((), ()))

X, Z, CORES = 4, 8, 2
ROW = X * CORES
LON = 8
RING = 2 * Z
BLOCKS, SLOTS, BLOCK, LANES = 24, 8, 512, 128
Q = BLOCK // LANES
INNER = BLOCKS * Q
RIM = INNER // 2
EXT = INNER + 2 * RIM
PART = EXT // ROW
CHUNK = 8
CHUNKS = BLOCKS // CHUNK
CROWS = CHUNK * Q
MEMBERS = X * Z * CORES


def kernel(
    ens, inc, off, tap_hbm, out,
    ebuf, dbuf, ring, yhalo, incf, mu, muin, delta, w, wd, tap, outf, outb, red,
    tsem, es, er, hs, hr, fs, fr, rs, rr, ls, lr, ys, yr, ms, mr, ds_, dr, os_, or_,
):
    lon, mem = lax.axis_index("lon"), lax.axis_index("mem")
    x, zlo, core = mem // (Z * CORES), (mem // CORES) % Z, mem % CORES
    y, zhi = lon // 2, lon % 2
    r = x * CORES + core
    z = zhi * Z + zlo

    def row_peer(d):
        rr_ = (r + d) % ROW
        return (lon, (rr_ // CORES) * (Z * CORES) + zlo * CORES + rr_ % CORES)

    def col_peer(d):
        return (lon, x * (Z * CORES) + ((zlo + d) % Z) * CORES + core)

    def ring_peer(d):
        zz = (z + d + RING) % RING
        return (y * 2 + zz // Z, x * (Z * CORES) + (zz % Z) * CORES + core)

    def lon_peer(d):
        return ((lon + d + LON) % LON, mem)

    y_to = lon_peer(2 - 4 * zhi)

    def copy(src, dst, ssem, rsem, dev):
        return pltpu.make_async_remote_copy(
            src_ref=src, dst_ref=dst, send_sem=ssem, recv_sem=rsem,
            device_id=dev, device_id_type=MESH,
        )

    tap_copy = pltpu.make_async_copy(tap_hbm, tap, tsem)
    tap_copy.start()

    barrier = pltpu.get_barrier_semaphore()
    peers = [row_peer(d) for d in range(1, ROW)] + [col_peer(d) for d in range(1, Z)]
    peers += [ring_peer(1), ring_peer(-1)]
    peers += [lon_peer(d) for d in (1, -1, 2, -2)]
    for dev in peers:
        pl.semaphore_signal(barrier, inc=1, device_id=dev, device_id_type=MESH)
    pl.semaphore_wait(barrier, len(peers))

    def erow(row, lo, n):
        return ebuf.at[pl.ds(pl.multiple_of(row * EXT + lo, 8), n)]

    halo_lo = copy(ens.at[pl.ds(RIM, RIM)], erow(r, 0, RIM), hs.at[0], hr.at[0], lon_peer(1))
    halo_hi = copy(ens.at[pl.ds(0, RIM)], erow(r, RIM + INNER, RIM), hs.at[1], hr.at[1], lon_peer(-1))
    halo_lo.start()
    halo_hi.start()

    def right(t):
        slot = (z - t + RING) % RING
        src = inc if t == 0 else ring.at[slot]
        return copy(src, ring.at[slot], rs.at[t], rr.at[t], ring_peer(1))

    def left(t):
        slot = (z + t) % RING
        src = inc if t == 0 else ring.at[slot]
        return copy(src, ring.at[slot], ls.at[t], lr.at[t], ring_peer(-1))

    right(0).start()
    left(0).start()
    inner = [copy(ens, erow(r, RIM, INNER), es.at[d], er.at[d], row_peer(d)) for d in range(1, ROW)]
    for c in inner:
        c.start()
    ebuf[pl.ds(pl.multiple_of(r * EXT + RIM, 8), INNER), :] = ens[...]
    ring[z] = inc[...]

    fwd = []
    for side, lo in ((0, 0), (1, RIM + INNER)):
        for d in range(1, ROW):
            fwd.append(copy(erow(r, lo, RIM), erow(r, lo, RIM), fs.at[side, d], fr.at[side, d], row_peer(d)))

    y_lo = pl.multiple_of((1 - zhi) * RIM, 16)

    def y_copy(k, slot):
        return copy(ring.at[slot, pl.ds(y_lo, RIM)], yhalo.at[k], ys.at[k], yr.at[k], y_to)

    def on_y(slot):
        @pl.when(slot // Z != zhi)
        def _():
            y_copy(slot % Z, slot).start()

    for t in range(RING // 2):
        slot = (z - 1 - t + RING) % RING
        copy(ring.at[slot], ring.at[slot], rs.at[t], rr.at[t], ring_peer(1)).wait_recv()
        if t < RING // 2 - 1:
            right(t + 1).start()
        on_y(slot)
        if t < RING // 2 - 1:
            slot = (z + 1 + t) % RING
            copy(ring.at[slot], ring.at[slot], ls.at[t], lr.at[t], ring_peer(-1)).wait_recv()
            if t < RING // 2 - 2:
                left(t + 1).start()
            on_y(slot)
        if t == 2:
            halo_lo.wait_recv()
            for c in fwd[: ROW - 1]:
                c.start()
            halo_hi.wait_recv()
            for c in fwd[ROW - 1 :]:
                c.start()

    for d in range(1, ROW):
        src = (r - d + ROW) % ROW
        copy(ens, erow(src, RIM, INNER), es.at[d], er.at[d], row_peer(d)).wait_recv()
        for side, lo in ((0, 0), (1, RIM + INNER)):
            copy(erow(src, lo, RIM), erow(src, lo, RIM), fs.at[side, d], fr.at[side, d], row_peer(d)).wait_recv()

    step = 32

    def differences(i, _):
        at = pl.multiple_of(i * step, step)
        rows = [ebuf[pl.ds(pl.multiple_of(m * EXT + at, 8), step), :] for m in range(ROW)]
        mean = functools.reduce(jnp.add, rows) * (1.0 / ROW)
        mu[pl.ds(at, step), :] = mean
        for m in range(ROW):
            dbuf[pl.ds(pl.multiple_of(m * EXT + at, 8), step), :] = rows[m] - mean
        return 0

    lax.fori_loop(0, EXT // step, differences, 0)

    part = pl.multiple_of(r * PART, 8)
    means = [copy(mu.at[pl.ds(part, PART)], muin.at[zlo], ms.at[d], mr.at[d], col_peer(d)) for d in range(1, Z)]
    for c in means:
        c.start()
    muin[zlo] = mu[pl.ds(part, PART), :]

    def widen(k, _):
        base = k * EXT
        incf[pl.ds(pl.multiple_of(base + RIM, 8), INNER), :] = ring[zhi * Z + k].astype(F32)
        near = pl.multiple_of(base + (1 - zhi) * (RIM + INNER), 8)
        incf[pl.ds(near, RIM), :] = ring[(1 - zhi) * Z + k, pl.ds(pl.multiple_of(zhi * RIM, 16), RIM), :].astype(F32)
        return 0

    lax.fori_loop(0, Z, widen, 0)
    for k in range(Z):
        y_copy(k, k).wait_recv()

    def widen_y(k, _):
        far = pl.multiple_of(k * EXT + zhi * (RIM + INNER), 8)
        incf[pl.ds(far, RIM), :] = yhalo[k].astype(F32)
        return 0

    lax.fori_loop(0, Z, widen_y, 0)

    def weigh(j, _):
        for q in range(Q):
            dq = dbuf[pl.ds(j * Q + q, ROW, stride=EXT), :]
            iq = incf[pl.ds(j * Q + q, Z, stride=EXT), :]
            rows = jnp.concatenate([dq[m : m + 1] * iq for m in range(ROW)], axis=0)
            w[j, :, q * LANES : (q + 1) * LANES] = rows.astype(BF16)
        return 0

    lax.fori_loop(0, 2 * BLOCKS, weigh, 0)

    for d in range(1, Z):
        src = (zlo - d + Z) % Z
        copy(mu.at[pl.ds(part, PART)], muin.at[src], ms.at[d], mr.at[d], col_peer(d)).wait_recv()
    total = functools.reduce(jnp.add, [muin[k] for k in range(Z)])
    delta[pl.ds(part, PART), :] = mu[pl.ds(part, PART), :] - total * (1.0 / Z)
    shifts = [copy(delta.at[pl.ds(part, PART)], delta.at[pl.ds(part, PART)], ds_.at[d], dr.at[d], row_peer(d)) for d in range(1, ROW)]
    for c in shifts:
        c.start()
    tap_copy.wait()

    def block_of(i, s):
        j = i + BLOCKS // 2
        return j if s == 0 else j + off[i, s - 1]

    def shift_pass():
        for d in range(1, ROW):
            src = pl.multiple_of(((r - d + ROW) % ROW) * PART, 8)
            copy(delta.at[pl.ds(src, PART)], delta.at[pl.ds(src, PART)], ds_.at[d], dr.at[d], row_peer(d)).wait_recv()

        def weigh_shift(j, _):
            for q in range(Q):
                iq = incf[pl.ds(j * Q + q, Z, stride=EXT), :]
                wd[j, :, q * LANES : (q + 1) * LANES] = delta[pl.ds(j * Q + q, 1), :] * iq
            return 0

        lax.fori_loop(0, 2 * BLOCKS, weigh_shift, 0)
        acc = None
        for s in range(SLOTS):
            lhs = jnp.concatenate([wd[block_of(i, s)] for i in range(BLOCKS)], axis=0).astype(BF16)
            part_ = lax.dot_general(lhs, tap[s], NT, preferred_element_type=F32)
            acc = part_ if acc is None else acc + part_
        for i in range(BLOCKS):
            for q in range(Q):
                shift = delta[pl.ds(RIM + i * Q + q, 1), :] * float(ROW)
                outf[pl.ds(i * Q + q, Z, stride=INNER), :] = (
                    shift * acc[i * Z : (i + 1) * Z, q * LANES : (q + 1) * LANES]
                )

    def product(c, _):
        i0 = c * CHUNK
        acc = None
        for s in range(SLOTS):
            lhs = jnp.concatenate([w[block_of(i0 + b, s)] for b in range(CHUNK)], axis=0)
            part_ = lax.dot_general(lhs, tap[s], NT, preferred_element_type=F32)
            acc = part_ if acc is None else acc + part_

        pl.when(c == 0)(shift_pass)

        for b in range(CHUNK):
            for q in range(Q):
                at = (i0 + b) * Q + q
                dq = dbuf[pl.ds(RIM + at, ROW, stride=EXT), :]
                o = outf[pl.ds(at, Z, stride=INNER), :]
                for m in range(ROW):
                    lo = (b * ROW + m) * Z
                    o += dq[m : m + 1] * acc[lo : lo + Z, q * LANES : (q + 1) * LANES]
                outf[pl.ds(at, Z, stride=INNER), :] = o
        rows = pl.multiple_of(c * CROWS, CROWS)
        for k in range(Z):
            outb[k, pl.ds(rows, CROWS), :] = outf[pl.ds(pl.multiple_of(k * INNER + rows, 8), CROWS), :].astype(BF16)
        for d in range(1, Z):
            send(c, d).start()
        return 0

    def send(c, d):
        rows = pl.ds(pl.multiple_of(c * CROWS, CROWS), CROWS)
        return copy(outb.at[(zlo + d) % Z, rows], red.at[zlo, rows], os_.at[c, d], or_.at[c, d], col_peer(d))

    lax.fori_loop(0, CHUNKS, product, 0)

    own = outf[pl.ds(pl.multiple_of(zlo * INNER, 8), INNER), :]
    for d in range(1, Z):
        src = (zlo - d + Z) % Z
        for c in range(CHUNKS):
            rows = pl.ds(c * CROWS, CROWS)
            copy(outb.at[src, rows], red.at[src, rows], os_.at[c, d], or_.at[c, d], col_peer(d)).wait_recv()
        own += red[src].astype(F32)
    out[...] = own / (MEMBERS - 1)

    for c in [halo_lo, halo_hi] + inner + fwd + means + shifts:
        c.wait_send()
    for t in range(RING // 2):
        right(t).wait_send()
        if t < RING // 2 - 1:
            left(t).wait_send()
    for k in range(Z):
        y_copy(k, k).wait_send()
    for c in range(CHUNKS):
        for d in range(1, Z):
            send(c, d).wait_send()


def on_device(ensemble, increments, offsets, taper):
    ens = ensemble.reshape(INNER, LANES)
    inc = increments.reshape(INNER, LANES)
    dma = pltpu.SemaphoreType.DMA
    vmem = pl.BlockSpec(memory_space=pltpu.VMEM)
    out = pl.pallas_call(
        kernel,
        out_shape=jax.ShapeDtypeStruct((INNER, LANES), F32),
        in_specs=[vmem, vmem, pl.BlockSpec(memory_space=pltpu.SMEM), pl.BlockSpec(memory_space=pl.ANY)],
        out_specs=vmem,
        scratch_shapes=[
            pltpu.VMEM((ROW * EXT, LANES), F32),
            pltpu.VMEM((ROW * EXT, LANES), F32),
            pltpu.VMEM((RING, INNER, LANES), BF16),
            pltpu.VMEM((Z, RIM, LANES), BF16),
            pltpu.VMEM((Z * EXT, LANES), F32),
            pltpu.VMEM((EXT, LANES), F32),
            pltpu.VMEM((Z, PART, LANES), F32),
            pltpu.VMEM((EXT, LANES), F32),
            pltpu.VMEM((2 * BLOCKS, ROW * Z, BLOCK), BF16),
            pltpu.VMEM((2 * BLOCKS, Z, BLOCK), F32),
            pltpu.VMEM((SLOTS, BLOCK, BLOCK), BF16),
            pltpu.VMEM((Z * INNER, LANES), F32),
            pltpu.VMEM((Z, INNER, LANES), BF16),
            pltpu.VMEM((Z, INNER, LANES), BF16),
            dma,
            dma((ROW,)), dma((ROW,)),
            dma((2,)), dma((2,)),
            dma((2, ROW)), dma((2, ROW)),
            dma((RING // 2,)), dma((RING // 2,)),
            dma((RING // 2,)), dma((RING // 2,)),
            dma((Z,)), dma((Z,)),
            dma((Z,)), dma((Z,)),
            dma((ROW,)), dma((ROW,)),
            dma((CHUNKS, Z)), dma((CHUNKS, Z)),
        ],
        compiler_params=pltpu.CompilerParams(
            collective_id=0, has_side_effects=True, vmem_limit_bytes=48 << 20
        ),
        name="covariance",
    )(ens, inc, offsets, taper)
    return out.reshape(1, INNER * LANES)


def solution(mesh):
    return jax.shard_map(
        on_device,
        mesh=mesh,
        in_specs=(P("mem", "lon"), P("mem", "lon"), P("lon", None), P()),
        out_specs=P("mem", "lon"),
        check_vma=False,
    )
```

```python
import functools

import jax
import jax.numpy as jnp
from jax import lax
from jax.experimental import pallas as pl
from jax.experimental.pallas import tpu as pltpu
from jax.sharding import PartitionSpec as P

MESH = pl.DeviceIdType.MESH
F32, BF16 = jnp.float32, jnp.bfloat16
NT = (((1,), (1,)), ((), ()))

X, Z, CORES = 4, 8, 2
ROW = X * CORES
HALF = Z // 2
LON = 8
RING = 2 * Z
BLOCKS, SLOTS, BLOCK, LANES = 24, 8, 512, 128
Q = BLOCK // LANES
INNER = BLOCKS * Q
RIM = INNER // 2
EXT = INNER + 2 * RIM
PART = 16
PARTS = INNER // PART
CHUNK = 8
CHUNKS = BLOCKS // CHUNK
CROWS = CHUNK * Q
MEMBERS = X * Z * CORES


def kernel(
    ens, inc, off, tap_hbm, out,
    eb, ib, db, incf, df, mus, mi, dsend, dlt, w, wd, tap, outf, outb, red,
    hello, tsem, es, er, is_, ir, hs, hr, fs, fr, ds_, dr, ms, mr, ss, sr, bs, br, os_, or_,
):
    lon, mem = lax.axis_index("lon"), lax.axis_index("mem")
    x, zlo, core = mem // (Z * CORES), (mem // CORES) % Z, mem % CORES
    zhi = lon % 2
    r = x * CORES + core
    g = x * 2 + zlo % 2
    zq = zlo // 2
    mine = core * HALF + zq

    def rank(zz):
        return jnp.minimum(zz, Z)

    rank_me = rank(zhi * Z + zlo)

    def row_peer(d):
        rr_ = (r + d) % ROW
        return (lon, (rr_ // CORES) * (Z * CORES) + zlo * CORES + rr_ % CORES)

    def set_peer(d):
        gg = (g + d) % ROW
        return (lon, (gg // 2) * (Z * CORES) + (zq * 2 + gg % 2) * CORES + core)

    def far_peer(dl, d):
        zt = (zlo + d) % Z
        half = zhi if dl == 0 else 1 - zhi
        dev = ((lon + dl + LON) % LON, x * (Z * CORES) + zt * CORES + core)
        return dev, rank(half * Z + zt)

    far = [(dl, d, *far_peer(dl, d)) for dl in (0, 1, -1) for d in range(Z) if dl or d]

    def copy(src, dst, ssem, rsem, dev):
        return pltpu.make_async_remote_copy(
            src_ref=src, dst_ref=dst, send_sem=ssem, recv_sem=rsem,
            device_id=dev, device_id_type=MESH,
        )

    tap_copy = pltpu.make_async_copy(tap_hbm, tap, tsem)
    tap_copy.start()

    barrier = pltpu.get_barrier_semaphore()
    for d in range(1, ROW):
        pl.semaphore_signal(barrier, inc=1, device_id=row_peer(d), device_id_type=MESH)
    for d in range(1, ROW):
        pl.semaphore_signal(barrier, inc=1, device_id=set_peer(d), device_id_type=MESH)
    before, after = 2 * (ROW - 1), [0, 0]
    for dl, _, dev, rk in far:

        @pl.when(rk >= rank_me)
        def _():
            pl.semaphore_signal(barrier, inc=1, device_id=dev, device_id_type=MESH)

        before += (rk <= rank_me).astype(jnp.int32)
        after[abs(dl)] += (rk > rank_me).astype(jnp.int32)
    pl.semaphore_wait(barrier, before)
    for dl, _, dev, rk in far:

        @pl.when(rk < rank_me)
        def _():
            pl.semaphore_signal(hello.at[abs(dl)], inc=1, device_id=dev, device_id_type=MESH)

    def wait_hello(n):
        pl.when(after[n] > 0)(lambda: pl.semaphore_wait(hello.at[n], after[n]))

    def ecopy(d, src):
        return copy(ens, eb.at[src], es.at[d], er.at[d], row_peer(d))

    def icopy(d, src):
        return copy(inc, ib.at[src, pl.ds(RIM, INNER)], is_.at[d], ir.at[d], set_peer(d))

    def ihalo(dl):
        n, lo, to = (0, RIM, 0) if dl == 1 else (1, 0, RIM + INNER)
        return copy(inc.at[pl.ds(lo, RIM)], ib.at[g, pl.ds(to, RIM)], hs.at[n], hr.at[n], far_peer(dl, 0)[0])

    def ifwd(n, d, src):
        rim = ib.at[src, pl.ds(n * (RIM + INNER), RIM)]
        return copy(rim, rim, fs.at[n, d], fr.at[n, d], set_peer(d))

    def dcopy(dl, d, src, dev):
        n, lo, to, rows = {0: (0, RIM, RIM, INNER), 1: (1, 2 * RIM, 0, RIM), -1: (2, RIM, RIM + INNER, RIM)}[dl]
        row = core * HALF + src
        return copy(db.at[row, pl.ds(lo, rows)], db.at[row, pl.ds(to, rows)], ds_.at[n, d // 2], dr.at[n, src], dev)

    def bcopy(n, side):
        lo, rows = ((RIM, INNER), (0, RIM), (RIM + INNER, RIM))[n]
        half = db.at[pl.ds(side * HALF, HALF), pl.ds(lo, rows)]
        return copy(half, half, bs.at[n], br.at[n], (lon, mem + 1 - 2 * core))

    part = pl.multiple_of((r % PARTS) * PART, PART)

    def mcopy(n, d, src, dev):
        return copy(mus.at[pl.ds(part, PART)], mi.at[n, src], ms.at[n, d], mr.at[n, src], dev)

    has_part = {0: r < PARTS, 1: (r >= PARTS // 2) & (r < PARTS), -1: r < PARTS // 2}

    def scopy(d, src):
        there = pl.ds(pl.multiple_of(((r + d) % ROW // CORES * 2 + zlo % 2) * 2 * PART, 2 * PART), 2 * PART)
        here = pl.ds(pl.multiple_of((src % PARTS) * 2 * PART, 2 * PART), 2 * PART)
        return copy(dsend.at[there], dlt.at[here], ss.at[d], sr.at[src], row_peer(d))

    def ocopy(c, d, src):
        rows = pl.ds(pl.multiple_of(c * CROWS, CROWS), CROWS)
        return copy(outb.at[(g + d) % ROW, rows], red.at[src, rows], os_.at[c, d], or_.at[c, src], set_peer(d))

    for d in range(1, ROW):
        ecopy(d, r).start()
    for dl in (1, -1):
        pl.when(far_peer(dl, 0)[1] <= rank_me)(lambda dl=dl: ihalo(dl).start())
    for d in range(1, ROW):
        icopy(d, g).start()
    eb[r] = ens[...]
    ib[g, pl.ds(RIM, INNER), :] = inc[...]

    for d in range(1, ROW):
        ecopy(d, (r - d + ROW) % ROW).wait_recv()
    mean = functools.reduce(jnp.add, [eb[k] for k in range(ROW)]) * (1.0 / ROW)
    mus[...] = mean
    db[mine, pl.ds(RIM, INNER), :] = (ens[...] - mean).astype(BF16)

    def send_far(late, dls):
        def due(rk):
            return (rk > rank_me) if late else (rk <= rank_me)

        for dl, d, dev, rk in far:
            if dl in dls and d % 2 == 0:
                pl.when(due(rk))(lambda: dcopy(dl, d, zq, dev).start())
        for dl, d, dev, rk in far:
            if dl in dls:
                pl.when(due(rk) & has_part[dl])(lambda: mcopy(abs(dl), d, zlo, dev).start())

    send_far(False, (1, -1))
    send_far(False, (0,))
    wait_hello(0)
    send_far(True, (0,))
    wait_hello(1)
    for dl in (1, -1):
        pl.when(far_peer(dl, 0)[1] > rank_me)(lambda dl=dl: ihalo(dl).start())
    send_far(True, (1, -1))

    @pl.when(has_part[0])
    def _():
        mi[0, zlo] = mus[pl.ds(part, PART), :]

    ihalo(1).wait_recv()
    for d in range(1, ROW):
        ifwd(0, d, g).start()
    ihalo(-1).wait_recv()
    for d in range(1, ROW):
        ifwd(1, d, g).start()
    for k in range(HALF):
        pl.when(k != zq)(lambda k=k: dcopy(0, 0, k, far[0][2]).wait_recv())
    bcopy(0, core).start()
    for d in range(1, ROW):
        icopy(d, (g - d + ROW) % ROW).wait_recv()
    tap_copy.wait()
    for n in range(2):
        for d in range(1, ROW):
            ifwd(n, d, (g - d + ROW) % ROW).wait_recv()

    def widen(src, dst, lo, n):
        def one(k, _):
            dst[pl.ds(pl.multiple_of(k * EXT, EXT), EXT), :] = src[k].astype(F32)
            return 0

        lax.fori_loop(lo, lo + n, one, 0)

    widen(ib, incf, 0, ROW)
    for dl in (1, -1):
        for k in range(HALF):
            dcopy(dl, 0, k, far[0][2]).wait_recv()
        bcopy(1 if dl == 1 else 2, core).start()
    widen(db, df, core * HALF, HALF)
    for n in range(3):
        bcopy(n, 1 - core).wait_recv()
    widen(db, df, (1 - core) * HALF, HALF)

    @pl.when(has_part[0])
    def _():
        for k in range(Z):
            pl.when(k != zlo)(lambda k=k: mcopy(0, 0, k, far[0][2]).wait_recv())
            mcopy(1, 0, k, far[0][2]).wait_recv()
        for n in range(2):
            whole = functools.reduce(jnp.add, [mi[n, k] for k in range(Z)]) * (1.0 / Z)
            for k in range(Z):
                dsend[k * 2 * PART + n * PART : k * 2 * PART + (n + 1) * PART, :] = mi[n, k] - whole
        here = pl.ds(pl.multiple_of((r % PARTS) * 2 * PART, 2 * PART), 2 * PART)
        dlt[here, :] = dsend[pl.ds(pl.multiple_of(g * 2 * PART, 2 * PART), 2 * PART), :]
        for d in range(1, ROW):
            scopy(d, r).start()

    def weigh(j, _):
        for q in range(Q):
            dq = df[pl.ds(j * Q + q, Z, stride=EXT), :]
            iq = incf[pl.ds(j * Q + q, ROW, stride=EXT), :]
            rows = jnp.concatenate([dq[m : m + 1] * iq for m in range(Z)], axis=0)
            w[j, :, q * LANES : (q + 1) * LANES] = rows.astype(BF16)
        return 0

    lax.fori_loop(0, 2 * BLOCKS, weigh, 0)

    def shift_row(j, q):
        b = (j + BLOCKS // 2) % BLOCKS
        rim = (j < BLOCKS // 2) | (j >= BLOCKS + BLOCKS // 2)
        rim = int(rim) if isinstance(j, int) else rim.astype(jnp.int32)
        return (b // Q) * 2 * PART + rim * PART + (b % Q) * Q + q

    def block_of(i, s):
        j = i + BLOCKS // 2
        return j if s == 0 else j + off[s - 1, i]

    def shift_pass():
        for k in range(PARTS):
            pl.when(k != r)(lambda k=k: scopy(1, k).wait_recv())

        def weigh_shift(j, _):
            for q in range(Q):
                iq = incf[pl.ds(j * Q + q, ROW, stride=EXT), :]
                wd[j, :, q * LANES : (q + 1) * LANES] = dlt[pl.ds(shift_row(j, q), 1), :] * iq
            return 0

        lax.fori_loop(0, 2 * BLOCKS, weigh_shift, 0)
        acc = None
        for s in range(SLOTS):
            lhs = jnp.concatenate([wd[block_of(i, s)] for i in range(BLOCKS)], axis=0).astype(BF16)
            part_ = lax.dot_general(lhs, tap[s], NT, preferred_element_type=F32)
            acc = part_ if acc is None else acc + part_
        for i in range(BLOCKS):
            for q in range(Q):
                shift = dlt[pl.ds(shift_row(i + BLOCKS // 2, q), 1), :] * float(ROW)
                outf[pl.ds(i * Q + q, ROW, stride=INNER), :] = (
                    shift * acc[i * ROW : (i + 1) * ROW, q * LANES : (q + 1) * LANES]
                )

    def product(c, _):
        i0 = c * CHUNK
        acc = None
        for s in range(SLOTS):
            lhs = jnp.concatenate([w[block_of(i0 + b, s)] for b in range(CHUNK)], axis=0)
            part_ = lax.dot_general(lhs, tap[s], NT, preferred_element_type=F32)
            acc = part_ if acc is None else acc + part_

        pl.when(c == 0)(shift_pass)

        for b in range(CHUNK):
            for q in range(Q):
                at = (i0 + b) * Q + q
                dq = df[pl.ds(RIM + at, Z, stride=EXT), :]
                o = outf[pl.ds(at, ROW, stride=INNER), :]
                for m in range(Z):
                    lo = (b * Z + m) * ROW
                    o += dq[m : m + 1] * acc[lo : lo + ROW, q * LANES : (q + 1) * LANES]
                outf[pl.ds(at, ROW, stride=INNER), :] = o
        rows = pl.multiple_of(c * CROWS, CROWS)
        for k in range(ROW):
            outb[k, pl.ds(rows, CROWS), :] = outf[pl.ds(pl.multiple_of(k * INNER + rows, 8), CROWS), :].astype(BF16)
        for d in range(1, ROW):
            ocopy(c, d, g).start()
        return 0

    lax.fori_loop(0, CHUNKS, product, 0)

    own = outf[pl.ds(pl.multiple_of(g * INNER, 8), INNER), :]
    for d in range(1, ROW):
        src = (g - d + ROW) % ROW
        for c in range(CHUNKS):
            ocopy(c, d, src).wait_recv()
        own += red[src].astype(F32)
    out[...] = own / (MEMBERS - 1)

    for d in range(1, ROW):
        ecopy(d, r).wait_send()
        icopy(d, g).wait_send()
        for n in range(2):
            ifwd(n, d, g).wait_send()
        for c in range(CHUNKS):
            ocopy(c, d, g).wait_send()
    for dl in (1, -1):
        ihalo(dl).wait_send()
    for n in range(3):
        bcopy(n, core).wait_send()
    for dl, d, dev, _ in far:
        if d % 2 == 0:
            dcopy(dl, d, zq, dev).wait_send()
        pl.when(has_part[dl])(lambda: mcopy(abs(dl), d, zlo, dev).wait_send())

    @pl.when(has_part[0])
    def _():
        for d in range(1, ROW):
            scopy(d, r).wait_send()


def on_device(ensemble, increments, offsets, taper):
    ens = ensemble.reshape(INNER, LANES)
    inc = increments.reshape(INNER, LANES)
    dma = pltpu.SemaphoreType.DMA
    vmem = pl.BlockSpec(memory_space=pltpu.VMEM)
    out = pl.pallas_call(
        kernel,
        out_shape=jax.ShapeDtypeStruct((INNER, LANES), F32),
        in_specs=[vmem, vmem, pl.BlockSpec(memory_space=pltpu.SMEM), pl.BlockSpec(memory_space=pltpu.HBM)],
        out_specs=vmem,
        scratch_shapes=[
            pltpu.VMEM((ROW, INNER, LANES), F32),
            pltpu.VMEM((ROW, EXT, LANES), BF16),
            pltpu.VMEM((Z, EXT, LANES), BF16),
            pltpu.VMEM((ROW * EXT, LANES), F32),
            pltpu.VMEM((Z * EXT, LANES), F32),
            pltpu.VMEM((INNER, LANES), F32),
            pltpu.VMEM((2, Z, PART, LANES), F32),
            pltpu.VMEM((Z * 2 * PART, LANES), F32),
            pltpu.VMEM((PARTS * 2 * PART, LANES), F32),
            pltpu.VMEM((2 * BLOCKS, Z * ROW, BLOCK), BF16),
            pltpu.VMEM((2 * BLOCKS, ROW, BLOCK), F32),
            pltpu.VMEM((SLOTS, BLOCK, BLOCK), BF16),
            pltpu.VMEM((ROW * INNER, LANES), F32),
            pltpu.VMEM((ROW, INNER, LANES), BF16),
            pltpu.VMEM((ROW, INNER, LANES), BF16),
            pltpu.SemaphoreType.REGULAR((2,)),
            dma,
            dma((ROW,)), dma((ROW,)),
            dma((ROW,)), dma((ROW,)),
            dma((2,)), dma((2,)),
            dma((2, ROW)), dma((2, ROW)),
            dma((3, HALF)), dma((3, HALF)),
            dma((2, Z)), dma((2, Z)),
            dma((ROW,)), dma((ROW,)),
            dma((3,)), dma((3,)),
            dma((CHUNKS, ROW)), dma((CHUNKS, ROW)),
        ],
        compiler_params=pltpu.CompilerParams(
            collective_id=0, has_side_effects=True, vmem_limit_bytes=121 << 19
        ),
        name="covariance",
    )(ens, inc, offsets.T, taper)
    return out.reshape(1, INNER * LANES)


def solution(mesh):
    return jax.shard_map(
        on_device,
        mesh=mesh,
        in_specs=(P("mem", "lon"), P("mem", "lon"), P("lon", None), P()),
        out_specs=P("mem", "lon"),
        check_vma=False,
    )
```

```python
import functools

import jax
import jax.numpy as jnp
from jax import lax
from jax.experimental import pallas as pl
from jax.experimental.pallas import tpu as pltpu
from jax.sharding import PartitionSpec as P

MESH = pl.DeviceIdType.MESH
F32, BF16 = jnp.float32, jnp.bfloat16
NT = (((1,), (1,)), ((), ()))

X, Z, CORES = 4, 8, 2
ROW = X * CORES
HALF = Z // 2
LON = 8
RING = 2 * Z
BLOCKS, SLOTS, BLOCK, LANES = 24, 8, 512, 128
Q = BLOCK // LANES
INNER = BLOCKS * Q
RIM = INNER // 2
EXT = INNER + 2 * RIM
PART = 16
PARTS = INNER // PART
CHUNK = 8
CHUNKS = BLOCKS // CHUNK
CROWS = CHUNK * Q
MEMBERS = X * Z * CORES


def kernel(
    ens, inc, off, tap_hbm, out,
    eb, ib, db, incf, df, mus, mi, dsend, dlt, w, wd, tacc, tap, outf, outb, red,
    hello, tsem, es, er, is_, ir, hs, hr, fs, fr, ds_, dr, ms, mr, ss, sr, bs, br, os_, or_,
):
    lon, mem = lax.axis_index("lon"), lax.axis_index("mem")
    x, zlo, core = mem // (Z * CORES), (mem // CORES) % Z, mem % CORES
    zhi = lon % 2
    r = x * CORES + core
    g = x * 2 + zlo % 2
    zq = zlo // 2
    mine = core * HALF + zq

    def rank(zz):
        return jnp.minimum(zz, Z)

    rank_me = rank(zhi * Z + zlo)

    def row_peer(d):
        rr_ = (r + d) % ROW
        return (lon, (rr_ // CORES) * (Z * CORES) + zlo * CORES + rr_ % CORES)

    def set_peer(d):
        gg = (g + d) % ROW
        return (lon, (gg // 2) * (Z * CORES) + (zq * 2 + gg % 2) * CORES + core)

    def far_peer(dl, d):
        zt = (zlo + d) % Z
        half = zhi if dl == 0 else 1 - zhi
        dev = ((lon + dl + LON) % LON, x * (Z * CORES) + zt * CORES + core)
        return dev, rank(half * Z + zt)

    far = [(dl, d, *far_peer(dl, d)) for dl in (0, 1, -1) for d in range(Z) if dl or d]

    def copy(src, dst, ssem, rsem, dev):
        return pltpu.make_async_remote_copy(
            src_ref=src, dst_ref=dst, send_sem=ssem, recv_sem=rsem,
            device_id=dev, device_id_type=MESH,
        )

    tap_copy = pltpu.make_async_copy(tap_hbm, tap, tsem)
    tap_copy.start()

    barrier = pltpu.get_barrier_semaphore()
    for d in range(1, ROW):
        pl.semaphore_signal(barrier, inc=1, device_id=row_peer(d), device_id_type=MESH)
    for k in range(X):
        dev = (lon, k * (Z * CORES) + (zq * 2 + 1 - zlo % 2) * CORES + core)
        pl.semaphore_signal(barrier, inc=1, device_id=dev, device_id_type=MESH)
    before, after = ROW - 1 + X, [0, 0]
    for dl, _, dev, rk in far:

        @pl.when(rk >= rank_me)
        def _():
            pl.semaphore_signal(barrier, inc=1, device_id=dev, device_id_type=MESH)

        before += (rk <= rank_me).astype(jnp.int32)
        after[abs(dl)] += (rk > rank_me).astype(jnp.int32)
    pl.semaphore_wait(barrier, before)
    def wait_hello(n):
        pl.when(after[n] > 0)(lambda: pl.semaphore_wait(hello.at[n], after[n]))

    def ecopy(d, src):
        return copy(ens, eb.at[src], es.at[d], er.at[d], row_peer(d))

    def icopy(d, src):
        return copy(inc, ib.at[src, pl.ds(RIM, INNER)], is_.at[d], ir.at[d], set_peer(d))

    def ihalo(dl):
        n, lo, to = (0, RIM, 0) if dl == 1 else (1, 0, RIM + INNER)
        return copy(inc.at[pl.ds(lo, RIM)], ib.at[g, pl.ds(to, RIM)], hs.at[n], hr.at[n], far_peer(dl, 0)[0])

    def ifwd(n, d, src):
        rim = ib.at[src, pl.ds(n * (RIM + INNER), RIM)]
        return copy(rim, rim, fs.at[n, d], fr.at[n, d], set_peer(d))

    def dcopy(dl, d, src, dev):
        n, lo, to, rows = {0: (0, RIM, RIM, INNER), 1: (1, 2 * RIM, 0, RIM), -1: (2, RIM, RIM + INNER, RIM)}[dl]
        row = core * HALF + src
        return copy(db.at[row, pl.ds(lo, rows)], db.at[row, pl.ds(to, rows)], ds_.at[n, d // 2], dr.at[n, src], dev)

    def bcopy(n, side):
        lo, rows = ((RIM, INNER), (0, RIM), (RIM + INNER, RIM))[n]
        half = db.at[pl.ds(side * HALF, HALF), pl.ds(lo, rows)]
        return copy(half, half, bs.at[n], br.at[n], (lon, mem + 1 - 2 * core))

    part = pl.multiple_of((r % PARTS) * PART, PART)

    def mcopy(n, d, src, dev):
        return copy(mus.at[pl.ds(part, PART)], mi.at[n, src], ms.at[n, d], mr.at[n, src], dev)

    has_part = {0: r < PARTS, 1: (r >= PARTS // 2) & (r < PARTS), -1: r < PARTS // 2}

    def scopy(d, src):
        there = pl.ds(pl.multiple_of(((r + d) % ROW // CORES * 2 + zlo % 2) * 2 * PART, 2 * PART), 2 * PART)
        here = pl.ds(pl.multiple_of((src % PARTS) * 2 * PART, 2 * PART), 2 * PART)
        return copy(dsend.at[there], dlt.at[here], ss.at[d], sr.at[src], row_peer(d))

    def ocopy(c, d, src):
        rows = pl.ds(pl.multiple_of(c * CROWS, CROWS), CROWS)
        return copy(outb.at[(g + d) % ROW, rows], red.at[src, rows], os_.at[c, d], or_.at[c, src], set_peer(d))

    for d in range(1, ROW):
        ecopy(d, r).start()
    for dl, _, dev, rk in far:

        @pl.when(rk < rank_me)
        def _():
            pl.semaphore_signal(hello.at[abs(dl)], inc=1, device_id=dev, device_id_type=MESH)
    for dl in (1, -1):
        pl.when(far_peer(dl, 0)[1] <= rank_me)(lambda dl=dl: ihalo(dl).start())
    for d in range(1, ROW):
        icopy(d, g).start()
    eb[r] = ens[...]
    ib[g, pl.ds(RIM, INNER), :] = inc[...]
    outf[...] = jnp.zeros_like(outf)

    for d in range(1, ROW):
        ecopy(d, (r - d + ROW) % ROW).wait_recv()
    mean = functools.reduce(jnp.add, [eb[k] for k in range(ROW)]) * (1.0 / ROW)
    mus[...] = mean
    db[mine, pl.ds(RIM, INNER), :] = (ens[...] - mean).astype(BF16)

    def send_far(late, dls):
        def due(rk):
            return (rk > rank_me) if late else (rk <= rank_me)

        for dl, d, dev, rk in far:
            if dl in dls and d % 2 == 0:
                pl.when(due(rk))(lambda: dcopy(dl, d, zq, dev).start())
        for dl, d, dev, rk in far:
            if dl in dls:
                pl.when(due(rk) & has_part[dl])(lambda: mcopy(abs(dl), d, zlo, dev).start())

    send_far(False, (1, -1))
    send_far(False, (0,))
    wait_hello(0)
    send_far(True, (0,))
    wait_hello(1)
    for dl in (1, -1):
        pl.when(far_peer(dl, 0)[1] > rank_me)(lambda dl=dl: ihalo(dl).start())
    send_far(True, (1, -1))

    @pl.when(has_part[0])
    def _():
        mi[0, zlo] = mus[pl.ds(part, PART), :]

    ihalo(1).wait_recv()
    for d in range(1, ROW):
        ifwd(0, d, g).start()
    ihalo(-1).wait_recv()
    for d in range(1, ROW):
        ifwd(1, d, g).start()
    for k in range(HALF):
        pl.when(k != zq)(lambda k=k: dcopy(0, 0, k, far[0][2]).wait_recv())
    bcopy(0, core).start()
    for d in range(1, ROW):
        icopy(d, (g - d + ROW) % ROW).wait_recv()
    tap_copy.wait()
    for n in range(2):
        for d in range(1, ROW):
            ifwd(n, d, (g - d + ROW) % ROW).wait_recv()

    def widen(src, dst, k0, n, lo, rows):
        def one(k, _):
            dst[pl.ds(pl.multiple_of(k * EXT + lo, PART), rows), :] = src[k, pl.ds(lo, rows), :].astype(F32)
            return 0

        lax.fori_loop(k0, k0 + n, one, 0)

    def weigh(j, _):
        for q in range(Q):
            dq = df[pl.ds(j * Q + q, ROW, stride=EXT), :]
            iq = incf[pl.ds(j * Q + q, ROW, stride=EXT), :]
            rows = jnp.concatenate([dq[m : m + 1] * iq for m in range(ROW)], axis=0)
            w[j, :, q * LANES : (q + 1) * LANES] = rows.astype(BF16)
        return 0

    widen(ib, incf, 0, ROW, 0, EXT)
    bcopy(0, 1 - core).wait_recv()
    widen(db, df, 0, ROW, RIM, INNER)
    lax.fori_loop(BLOCKS // 2, BLOCKS + BLOCKS // 2, weigh, 0)

    def block_of(i, s):
        j = i + BLOCKS // 2
        return j if s == 0 else j + off[s - 1, i]

    def through(first, count, s):
        lhs = jnp.concatenate([w[block_of(first + b, s)] for b in range(count)], axis=0)
        whole = lax.dot_general(lhs, tap[s], NT, preferred_element_type=F32)
        return whole.reshape(count, ROW * ROW, BLOCK)

    def own_tile(c, _):
        tacc[pl.ds(c * CHUNK, CHUNK)] = through(c * CHUNK, CHUNK, 0)
        return 0

    lax.fori_loop(0, CHUNKS, own_tile, 0)
    mid = range(CHUNK, 2 * CHUNK)
    late = []
    for s in range(1, SLOTS):
        inner = [i for i in mid if BLOCKS // 2 + 1 - s <= i <= BLOCKS // 2 + 6 - s]
        tacc[pl.ds(inner[0], len(inner))] += through(inner[0], len(inner), s)
        late += [(mid[0], inner[0] - mid[0], s), (inner[-1] + 1, mid[-1] - inner[-1], s)]

    for dl in (1, -1):
        for k in range(HALF):
            dcopy(dl, 0, k, far[0][2]).wait_recv()
        bcopy(1 if dl == 1 else 2, core).start()
    widen(db, df, core * HALF, HALF, 0, RIM)
    widen(db, df, core * HALF, HALF, RIM + INNER, RIM)
    for n in (1, 2):
        bcopy(n, 1 - core).wait_recv()
        lo = (n - 1) * (RIM + INNER)
        widen(db, df, (1 - core) * HALF, HALF, lo, RIM)
        lax.fori_loop(lo // Q, lo // Q + BLOCKS // 2, weigh, 0)

    def shift_start():
        for k in range(Z):
            pl.when(k != zlo)(lambda k=k: mcopy(0, 0, k, far[0][2]).wait_recv())
            mcopy(1, 0, k, far[0][2]).wait_recv()
        for n in range(2):
            whole = functools.reduce(jnp.add, [mi[n, k] for k in range(Z)]) * (1.0 / Z)
            for k in range(Z):
                dsend[k * 2 * PART + n * PART : k * 2 * PART + (n + 1) * PART, :] = mi[n, k] - whole
        here = pl.ds(pl.multiple_of((r % PARTS) * 2 * PART, 2 * PART), 2 * PART)
        dlt[here, :] = dsend[pl.ds(pl.multiple_of(g * 2 * PART, 2 * PART), 2 * PART), :]
        for d in range(1, ROW):
            scopy(d, r).start()

    def shift_row(j, q):
        b = (j + BLOCKS // 2) % BLOCKS
        rim = (j < BLOCKS // 2) | (j >= BLOCKS + BLOCKS // 2)
        rim = int(rim) if isinstance(j, int) else rim.astype(jnp.int32)
        return (b // Q) * 2 * PART + rim * PART + (b % Q) * Q + q

    def shift_pass():
        for k in range(PARTS):
            pl.when(k != r)(lambda k=k: scopy(1, k).wait_recv())

        def weigh_shift(j, _):
            for q in range(Q):
                iq = incf[pl.ds(j * Q + q, ROW, stride=EXT), :]
                wd[j, :, q * LANES : (q + 1) * LANES] = dlt[pl.ds(shift_row(j, q), 1), :] * iq
            return 0

        lax.fori_loop(0, 2 * BLOCKS, weigh_shift, 0)
        acc = None
        for s in range(SLOTS):
            lhs = jnp.concatenate([wd[block_of(i, s)] for i in range(BLOCKS)], axis=0).astype(BF16)
            part_ = lax.dot_general(lhs, tap[s], NT, preferred_element_type=F32)
            acc = part_ if acc is None else acc + part_
        for i in range(BLOCKS):
            for q in range(Q):
                shift = dlt[pl.ds(shift_row(i + BLOCKS // 2, q), 1), :] * float(ROW)
                outf[pl.ds(i * Q + q, ROW, stride=INNER), :] += (
                    shift * acc[i * ROW : (i + 1) * ROW, q * LANES : (q + 1) * LANES]
                )

    def emit(c, _):
        rows = pl.multiple_of(c * CROWS, CROWS)
        for k in range(ROW):
            outb[k, pl.ds(rows, CROWS), :] = outf[pl.ds(pl.multiple_of(k * INNER + rows, 8), CROWS), :].astype(BF16)
        for d in range(1, ROW):
            ocopy(c, d, g).start()
        return 0

    def finish(c, acc):
        for b in range(CHUNK):
            for q in range(Q):
                at = (c * CHUNK + b) * Q + q
                dq = df[pl.ds(RIM + at, Z, stride=EXT), :]
                o = outf[pl.ds(at, ROW, stride=INNER), :]
                for m in range(Z):
                    lo = (b * Z + m) * ROW
                    o += dq[m : m + 1] * acc[lo : lo + ROW, q * LANES : (q + 1) * LANES]
                outf[pl.ds(at, ROW, stride=INNER), :] = o
    for first, count, s in late:
        if count:
            tacc[pl.ds(first, count)] += through(first, count, s)
    pl.when(has_part[0])(shift_start)
    finish(1, tacc[CHUNK : 2 * CHUNK].reshape(CHUNK * ROW * ROW, BLOCK))

    def product(n, _):
        c = n * 2
        acc = tacc[pl.ds(c * CHUNK, CHUNK)]
        for s in range(1, SLOTS):
            acc += through(c * CHUNK, CHUNK, s)

        @pl.when(n == 1)
        def _():
            shift_pass()
            lax.fori_loop(0, CHUNKS - 1, emit, 0)

        finish(c, acc.reshape(CHUNK * ROW * ROW, BLOCK))
        return 0

    lax.fori_loop(0, 2, product, 0)
    emit(CHUNKS - 1, 0)

    own = outf[pl.ds(pl.multiple_of(g * INNER, 8), INNER), :]
    for d in range(1, ROW):
        src = (g - d + ROW) % ROW
        for c in range(CHUNKS):
            ocopy(c, d, src).wait_recv()
        own += red[src].astype(F32)
    out[...] = own / (MEMBERS - 1)

    for d in range(1, ROW):
        ecopy(d, r).wait_send()
        icopy(d, g).wait_send()
        for n in range(2):
            ifwd(n, d, g).wait_send()
        for c in range(CHUNKS):
            ocopy(c, d, g).wait_send()
    for dl in (1, -1):
        ihalo(dl).wait_send()
    for n in range(3):
        bcopy(n, core).wait_send()
    for dl, d, dev, _ in far:
        if d % 2 == 0:
            dcopy(dl, d, zq, dev).wait_send()
        pl.when(has_part[dl])(lambda: mcopy(abs(dl), d, zlo, dev).wait_send())

    @pl.when(has_part[0])
    def _():
        for d in range(1, ROW):
            scopy(d, r).wait_send()


def on_device(ensemble, increments, offsets, taper):
    ens = ensemble.reshape(INNER, LANES)
    inc = increments.reshape(INNER, LANES)
    dma = pltpu.SemaphoreType.DMA
    vmem = pl.BlockSpec(memory_space=pltpu.VMEM)
    out = pl.pallas_call(
        kernel,
        out_shape=jax.ShapeDtypeStruct((INNER, LANES), F32),
        in_specs=[vmem, vmem, pl.BlockSpec(memory_space=pltpu.SMEM), pl.BlockSpec(memory_space=pltpu.HBM)],
        out_specs=vmem,
        scratch_shapes=[
            pltpu.VMEM((ROW, INNER, LANES), F32),
            pltpu.VMEM((ROW, EXT, LANES), BF16),
            pltpu.VMEM((Z, EXT, LANES), BF16),
            pltpu.VMEM((ROW * EXT, LANES), F32),
            pltpu.VMEM((Z * EXT, LANES), F32),
            pltpu.VMEM((INNER, LANES), F32),
            pltpu.VMEM((2, Z, PART, LANES), F32),
            pltpu.VMEM((Z * 2 * PART, LANES), F32),
            pltpu.VMEM((PARTS * 2 * PART, LANES), F32),
            pltpu.VMEM((2 * BLOCKS, Z * ROW, BLOCK), BF16),
            pltpu.VMEM((2 * BLOCKS, ROW, BLOCK), F32),
            pltpu.VMEM((BLOCKS, ROW * ROW, BLOCK), F32),
            pltpu.VMEM((SLOTS, BLOCK, BLOCK), BF16),
            pltpu.VMEM((ROW * INNER, LANES), F32),
            pltpu.VMEM((ROW, INNER, LANES), BF16),
            pltpu.VMEM((ROW, INNER, LANES), BF16),
            pltpu.SemaphoreType.REGULAR((2,)),
            dma,
            dma((ROW,)), dma((ROW,)),
            dma((ROW,)), dma((ROW,)),
            dma((2,)), dma((2,)),
            dma((2, ROW)), dma((2, ROW)),
            dma((3, HALF)), dma((3, HALF)),
            dma((2, Z)), dma((2, Z)),
            dma((ROW,)), dma((ROW,)),
            dma((3,)), dma((3,)),
            dma((CHUNKS, ROW)), dma((CHUNKS, ROW)),
        ],
        compiler_params=pltpu.CompilerParams(
            collective_id=0, has_side_effects=True, vmem_limit_bytes=121 << 19
        ),
        name="covariance",
    )(ens, inc, offsets.T, taper)
    return out.reshape(1, INNER * LANES)


def solution(mesh):
    return jax.shard_map(
        on_device,
        mesh=mesh,
        in_specs=(P("mem", "lon"), P("mem", "lon"), P("lon", None), P()),
        out_specs=P("mem", "lon"),
        check_vma=False,
    )
```

```python
import functools

import jax
import jax.numpy as jnp
from jax import lax
from jax.experimental import pallas as pl
from jax.experimental.pallas import tpu as pltpu
from jax.sharding import PartitionSpec as P

MESH = pl.DeviceIdType.MESH
F32, BF16 = jnp.float32, jnp.bfloat16
NT = (((1,), (1,)), ((), ()))

X, Z, CORES = 4, 8, 2
ROW = X * CORES
HALF = Z // 2
LON = 8
RING = 2 * Z
BLOCKS, SLOTS, BLOCK, LANES = 24, 8, 512, 128
Q = BLOCK // LANES
INNER = BLOCKS * Q
RIM = INNER // 2
EXT = INNER + 2 * RIM
PART = 16
PARTS = INNER // PART
CHUNK = 8
CHUNKS = BLOCKS // CHUNK
CROWS = CHUNK * Q
MEMBERS = X * Z * CORES


def kernel(
    ens, inc, off, tap_hbm, out,
    eb, ib, db, incf, df, mus, mi, dsend, dlt, w, wd, tacc, tap, outf, outb, red,
    hello, tsem, es, er, is_, ir, hs, hr, fs, fr, ds_, dr, ms, mr, ss, sr, bs, br, os_, or_,
):
    lon, mem = lax.axis_index("lon"), lax.axis_index("mem")
    x, zlo, core = mem // (Z * CORES), (mem // CORES) % Z, mem % CORES
    zhi = lon % 2
    r = x * CORES + core
    g = x * 2 + zlo % 2
    zq = zlo // 2
    mine = core * HALF + zq

    def rank(zz):
        return jnp.minimum(zz, Z)

    rank_me = rank(zhi * Z + zlo)

    def row_peer(d):
        rr_ = (r + d) % ROW
        return (lon, (rr_ // CORES) * (Z * CORES) + zlo * CORES + rr_ % CORES)

    def set_peer(d):
        gg = (g + d) % ROW
        return (lon, (gg // 2) * (Z * CORES) + (zq * 2 + gg % 2) * CORES + core)

    def far_peer(dl, d):
        zt = (zlo + d) % Z
        half = zhi if dl == 0 else 1 - zhi
        dev = ((lon + dl + LON) % LON, x * (Z * CORES) + zt * CORES + core)
        return dev, rank(half * Z + zt)

    far = [(dl, d, *far_peer(dl, d)) for dl in (0, 1, -1) for d in range(Z) if dl or d]

    def copy(src, dst, ssem, rsem, dev):
        return pltpu.make_async_remote_copy(
            src_ref=src, dst_ref=dst, send_sem=ssem, recv_sem=rsem,
            device_id=dev, device_id_type=MESH,
        )

    tap_copy = pltpu.make_async_copy(tap_hbm, tap, tsem)
    tap_copy.start()

    barrier = pltpu.get_barrier_semaphore()
    for d in range(1, ROW):
        pl.semaphore_signal(barrier, inc=1, device_id=row_peer(d), device_id_type=MESH)
    for k in range(X):
        dev = (lon, k * (Z * CORES) + (zq * 2 + 1 - zlo % 2) * CORES + core)
        pl.semaphore_signal(barrier, inc=1, device_id=dev, device_id_type=MESH)
    before, after = ROW - 1 + X, [0, 0]
    for dl, _, dev, rk in far:

        @pl.when(rk >= rank_me)
        def _():
            pl.semaphore_signal(barrier, inc=1, device_id=dev, device_id_type=MESH)

        before += (rk <= rank_me).astype(jnp.int32)
        after[abs(dl)] += (rk > rank_me).astype(jnp.int32)
    pl.semaphore_wait(barrier, before)
    def wait_hello(n):
        pl.when(after[n] > 0)(lambda: pl.semaphore_wait(hello.at[n], after[n]))

    def ecopy(d, src):
        return copy(ens, eb.at[src], es.at[d], er.at[d], row_peer(d))

    def icopy(d, src):
        return copy(inc, ib.at[src, pl.ds(RIM, INNER)], is_.at[d], ir.at[d], set_peer(d))

    def ihalo(dl):
        n, lo, to = (0, RIM, 0) if dl == 1 else (1, 0, RIM + INNER)
        return copy(inc.at[pl.ds(lo, RIM)], ib.at[g, pl.ds(to, RIM)], hs.at[n], hr.at[n], far_peer(dl, 0)[0])

    def ifwd(n, d, src):
        rim = ib.at[src, pl.ds(n * (RIM + INNER), RIM)]
        return copy(rim, rim, fs.at[n, d], fr.at[n, d], set_peer(d))

    def dcopy(dl, d, src, dev):
        n, lo, to, rows = {0: (0, RIM, RIM, INNER), 1: (1, 2 * RIM, 0, RIM), -1: (2, RIM, RIM + INNER, RIM)}[dl]
        row = core * HALF + src
        return copy(db.at[row, pl.ds(lo, rows)], db.at[row, pl.ds(to, rows)], ds_.at[n, d // 2], dr.at[n, src], dev)

    def bcopy(n, side):
        lo, rows = ((RIM, INNER), (0, RIM), (RIM + INNER, RIM))[n]
        half = db.at[pl.ds(side * HALF, HALF), pl.ds(lo, rows)]
        return copy(half, half, bs.at[n], br.at[n], (lon, mem + 1 - 2 * core))

    part = pl.multiple_of((r % PARTS) * PART, PART)

    def mcopy(n, d, src, dev):
        return copy(mus.at[pl.ds(part, PART)], mi.at[n, src], ms.at[n, d], mr.at[n, src], dev)

    has_part = {0: r < PARTS, 1: (r >= PARTS // 2) & (r < PARTS), -1: r < PARTS // 2}

    def scopy(d, src):
        there = pl.ds(pl.multiple_of(((r + d) % ROW // CORES * 2 + zlo % 2) * 2 * PART, 2 * PART), 2 * PART)
        here = pl.ds(pl.multiple_of((src % PARTS) * 2 * PART, 2 * PART), 2 * PART)
        return copy(dsend.at[there], dlt.at[here], ss.at[d], sr.at[src], row_peer(d))

    def ocopy(c, d, src):
        rows = pl.ds(pl.multiple_of(c * CROWS, CROWS), CROWS)
        return copy(outb.at[(g + d) % ROW, rows], red.at[src, rows], os_.at[c, d], or_.at[c, src], set_peer(d))

    for d in range(1, ROW):
        ecopy(d, r).start()
    for dl, _, dev, rk in far:

        @pl.when(rk < rank_me)
        def _():
            pl.semaphore_signal(hello.at[abs(dl)], inc=1, device_id=dev, device_id_type=MESH)
    for dl in (1, -1):
        pl.when(far_peer(dl, 0)[1] <= rank_me)(lambda dl=dl: ihalo(dl).start())
    for d in range(1, ROW):
        icopy(d, g).start()
    eb[r] = ens[...]
    ib[g, pl.ds(RIM, INNER), :] = inc[...]
    outf[...] = jnp.zeros_like(outf)

    for d in range(1, ROW):
        ecopy(d, (r - d + ROW) % ROW).wait_recv()
    mean = functools.reduce(jnp.add, [eb[k] for k in range(ROW)]) * (1.0 / ROW)
    mus[...] = mean
    db[mine, pl.ds(RIM, INNER), :] = (ens[...] - mean).astype(BF16)

    def send_far(late, dls):
        def due(rk):
            return (rk > rank_me) if late else (rk <= rank_me)

        for dl, d, dev, rk in far:
            if dl in dls:
                pl.when(due(rk) & has_part[dl])(lambda: mcopy(abs(dl), d, zlo, dev).start())
        for dl, d, dev, rk in far:
            if dl in dls and d % 2 == 0:
                pl.when(due(rk))(lambda: dcopy(dl, d, zq, dev).start())

    send_far(False, (1, -1))
    send_far(False, (0,))
    wait_hello(0)
    send_far(True, (0,))
    wait_hello(1)
    for dl in (1, -1):
        pl.when(far_peer(dl, 0)[1] > rank_me)(lambda dl=dl: ihalo(dl).start())
    send_far(True, (1, -1))

    @pl.when(has_part[0])
    def _():
        mi[0, zlo] = mus[pl.ds(part, PART), :]

    ihalo(1).wait_recv()
    for d in range(1, ROW):
        ifwd(0, d, g).start()
    ihalo(-1).wait_recv()
    for d in range(1, ROW):
        ifwd(1, d, g).start()
    for k in range(HALF):
        pl.when(k != zq)(lambda k=k: dcopy(0, 0, k, far[0][2]).wait_recv())
    bcopy(0, core).start()
    for d in range(1, ROW):
        icopy(d, (g - d + ROW) % ROW).wait_recv()
    tap_copy.wait()
    for n in range(2):
        for d in range(1, ROW):
            ifwd(n, d, (g - d + ROW) % ROW).wait_recv()

    def widen(src, dst, k0, n, lo, rows):
        def one(k, _):
            dst[pl.ds(pl.multiple_of(k * EXT + lo, PART), rows), :] = src[k, pl.ds(lo, rows), :].astype(F32)
            return 0

        lax.fori_loop(k0, k0 + n, one, 0)

    def weigh(j, _):
        for q in range(Q):
            dq = df[pl.ds(j * Q + q, ROW, stride=EXT), :]
            iq = incf[pl.ds(j * Q + q, ROW, stride=EXT), :]
            rows = jnp.concatenate([dq[m : m + 1] * iq for m in range(ROW)], axis=0)
            w[j, :, q * LANES : (q + 1) * LANES] = rows.astype(BF16)
        return 0

    widen(ib, incf, 0, ROW, 0, EXT)
    bcopy(0, 1 - core).wait_recv()
    widen(db, df, 0, ROW, RIM, INNER)
    lax.fori_loop(BLOCKS // 2, BLOCKS + BLOCKS // 2, weigh, 0)

    def block_of(i, s):
        j = i + BLOCKS // 2
        return j if s == 0 else j + off[s - 1, i]

    def through(first, count, s):
        lhs = jnp.concatenate([w[block_of(first + b, s)] for b in range(count)], axis=0)
        whole = lax.dot_general(lhs, tap[s], NT, preferred_element_type=F32)
        return whole.reshape(count, ROW * ROW, BLOCK)

    def own_tile(c, _):
        tacc[pl.ds(c * CHUNK, CHUNK)] = through(c * CHUNK, CHUNK, 0)
        return 0

    lax.fori_loop(0, CHUNKS, own_tile, 0)
    mid = range(CHUNK, 2 * CHUNK)
    late = []
    for s in range(1, SLOTS):
        inner = [i for i in mid if BLOCKS // 2 + 1 - s <= i <= BLOCKS // 2 + 6 - s]
        tacc[pl.ds(inner[0], len(inner))] += through(inner[0], len(inner), s)
        late += [(mid[0], inner[0] - mid[0], s), (inner[-1] + 1, mid[-1] - inner[-1], s)]

    def shift_start():
        for k in range(Z):
            pl.when(k != zlo)(lambda k=k: mcopy(0, 0, k, far[0][2]).wait_recv())
            mcopy(1, 0, k, far[0][2]).wait_recv()
        for n in range(2):
            whole = functools.reduce(jnp.add, [mi[n, k] for k in range(Z)]) * (1.0 / Z)
            for k in range(Z):
                dsend[k * 2 * PART + n * PART : k * 2 * PART + (n + 1) * PART, :] = mi[n, k] - whole
        here = pl.ds(pl.multiple_of((r % PARTS) * 2 * PART, 2 * PART), 2 * PART)
        dlt[here, :] = dsend[pl.ds(pl.multiple_of(g * 2 * PART, 2 * PART), 2 * PART), :]
        for d in range(1, ROW):
            scopy(d, r).start()

    def shift_row(j, q):
        b = (j + BLOCKS // 2) % BLOCKS
        rim = (j < BLOCKS // 2) | (j >= BLOCKS + BLOCKS // 2)
        rim = int(rim) if isinstance(j, int) else rim.astype(jnp.int32)
        return (b // Q) * 2 * PART + rim * PART + (b % Q) * Q + q

    def shift_pass():
        for k in range(PARTS):
            pl.when(k != r)(lambda k=k: scopy(1, k).wait_recv())

        def weigh_shift(j, _):
            for q in range(Q):
                iq = incf[pl.ds(j * Q + q, ROW, stride=EXT), :]
                wd[j, :, q * LANES : (q + 1) * LANES] = dlt[pl.ds(shift_row(j, q), 1), :] * iq
            return 0

        lax.fori_loop(0, 2 * BLOCKS, weigh_shift, 0)
        acc = None
        for s in range(SLOTS):
            lhs = jnp.concatenate([wd[block_of(i, s)] for i in range(BLOCKS)], axis=0).astype(BF16)
            part_ = lax.dot_general(lhs, tap[s], NT, preferred_element_type=F32)
            acc = part_ if acc is None else acc + part_
        for i in range(BLOCKS):
            for q in range(Q):
                shift = dlt[pl.ds(shift_row(i + BLOCKS // 2, q), 1), :] * float(ROW)
                outf[pl.ds(i * Q + q, ROW, stride=INNER), :] += (
                    shift * acc[i * ROW : (i + 1) * ROW, q * LANES : (q + 1) * LANES]
                )

    pl.when(has_part[0])(shift_start)
    for dl in (1, -1):
        for k in range(HALF):
            dcopy(dl, 0, k, far[0][2]).wait_recv()
        bcopy(1 if dl == 1 else 2, core).start()
    shift_pass()
    widen(db, df, core * HALF, HALF, 0, RIM)
    widen(db, df, core * HALF, HALF, RIM + INNER, RIM)
    for n in (1, 2):
        bcopy(n, 1 - core).wait_recv()
        lo = (n - 1) * (RIM + INNER)
        widen(db, df, (1 - core) * HALF, HALF, lo, RIM)
        lax.fori_loop(lo // Q, lo // Q + BLOCKS // 2, weigh, 0)

    def emit(c, _):
        rows = pl.multiple_of(c * CROWS, CROWS)
        for k in range(ROW):
            outb[k, pl.ds(rows, CROWS), :] = outf[pl.ds(pl.multiple_of(k * INNER + rows, 8), CROWS), :].astype(BF16)
        for d in range(1, ROW):
            ocopy(c, d, g).start()
        return 0

    def finish(c, acc):
        for b in range(CHUNK):
            for q in range(Q):
                at = (c * CHUNK + b) * Q + q
                dq = df[pl.ds(RIM + at, Z, stride=EXT), :]
                o = outf[pl.ds(at, ROW, stride=INNER), :]
                for m in range(Z):
                    lo = (b * Z + m) * ROW
                    o += dq[m : m + 1] * acc[lo : lo + ROW, q * LANES : (q + 1) * LANES]
                outf[pl.ds(at, ROW, stride=INNER), :] = o
    for first, count, s in late:
        if count:
            tacc[pl.ds(first, count)] += through(first, count, s)
    finish(1, tacc[CHUNK : 2 * CHUNK].reshape(CHUNK * ROW * ROW, BLOCK))
    emit(1, 0)

    def product(n, _):
        c = n * 2
        acc = tacc[pl.ds(c * CHUNK, CHUNK)]
        for s in range(1, SLOTS):
            acc += through(c * CHUNK, CHUNK, s)
        finish(c, acc.reshape(CHUNK * ROW * ROW, BLOCK))
        emit(c, 0)
        return 0

    lax.fori_loop(0, 2, product, 0)

    own = outf[pl.ds(pl.multiple_of(g * INNER, 8), INNER), :]
    for d in range(1, ROW):
        src = (g - d + ROW) % ROW
        for c in range(CHUNKS):
            ocopy(c, d, src).wait_recv()
        own += red[src].astype(F32)
    out[...] = own / (MEMBERS - 1)

    for d in range(1, ROW):
        ecopy(d, r).wait_send()
        icopy(d, g).wait_send()
        for n in range(2):
            ifwd(n, d, g).wait_send()
        for c in range(CHUNKS):
            ocopy(c, d, g).wait_send()
    for dl in (1, -1):
        ihalo(dl).wait_send()
    for n in range(3):
        bcopy(n, core).wait_send()
    for dl, d, dev, _ in far:
        if d % 2 == 0:
            dcopy(dl, d, zq, dev).wait_send()
        pl.when(has_part[dl])(lambda: mcopy(abs(dl), d, zlo, dev).wait_send())

    @pl.when(has_part[0])
    def _():
        for d in range(1, ROW):
            scopy(d, r).wait_send()


def on_device(ensemble, increments, offsets, taper):
    ens = ensemble.reshape(INNER, LANES)
    inc = increments.reshape(INNER, LANES)
    dma = pltpu.SemaphoreType.DMA
    vmem = pl.BlockSpec(memory_space=pltpu.VMEM)
    out = pl.pallas_call(
        kernel,
        out_shape=jax.ShapeDtypeStruct((INNER, LANES), F32),
        in_specs=[vmem, vmem, pl.BlockSpec(memory_space=pltpu.SMEM), pl.BlockSpec(memory_space=pltpu.HBM)],
        out_specs=vmem,
        scratch_shapes=[
            pltpu.VMEM((ROW, INNER, LANES), F32),
            pltpu.VMEM((ROW, EXT, LANES), BF16),
            pltpu.VMEM((Z, EXT, LANES), BF16),
            pltpu.VMEM((ROW * EXT, LANES), F32),
            pltpu.VMEM((Z * EXT, LANES), F32),
            pltpu.VMEM((INNER, LANES), F32),
            pltpu.VMEM((2, Z, PART, LANES), F32),
            pltpu.VMEM((Z * 2 * PART, LANES), F32),
            pltpu.VMEM((PARTS * 2 * PART, LANES), F32),
            pltpu.VMEM((2 * BLOCKS, Z * ROW, BLOCK), BF16),
            pltpu.VMEM((2 * BLOCKS, ROW, BLOCK), F32),
            pltpu.VMEM((BLOCKS, ROW * ROW, BLOCK), F32),
            pltpu.VMEM((SLOTS, BLOCK, BLOCK), BF16),
            pltpu.VMEM((ROW * INNER, LANES), F32),
            pltpu.VMEM((ROW, INNER, LANES), BF16),
            pltpu.VMEM((ROW, INNER, LANES), BF16),
            pltpu.SemaphoreType.REGULAR((2,)),
            dma,
            dma((ROW,)), dma((ROW,)),
            dma((ROW,)), dma((ROW,)),
            dma((2,)), dma((2,)),
            dma((2, ROW)), dma((2, ROW)),
            dma((3, HALF)), dma((3, HALF)),
            dma((2, Z)), dma((2, Z)),
            dma((ROW,)), dma((ROW,)),
            dma((3,)), dma((3,)),
            dma((CHUNKS, ROW)), dma((CHUNKS, ROW)),
        ],
        compiler_params=pltpu.CompilerParams(
            collective_id=0, has_side_effects=True, vmem_limit_bytes=121 << 19
        ),
        name="covariance",
    )(ens, inc, offsets.T, taper)
    return out.reshape(1, INNER * LANES)


def solution(mesh):
    return jax.shard_map(
        on_device,
        mesh=mesh,
        in_specs=(P("mem", "lon"), P("mem", "lon"), P("lon", None), P()),
        out_specs=P("mem", "lon"),
        check_vma=False,
    )
```
